256 devices in a mesh: rep: 32 (over z_lo, x, core), fsdp: 8 (over z_hi, y).
Axes of the slice: x: 4, y: 4, z: 8 (z_hi: 2, z_lo: 4; z = z_hi * 4 + z_lo), core: 2. Of those that a mesh axis runs over, the one named last changes fastest.
Arguments:
- activations: bfloat16 [32768, 3072], P(('rep', 'fsdp')), may hold values from -6 to 6
- targets: bfloat16 [32768, 6144], P('rep', 'fsdp'), may hold values from -16 to 16
- replica_weight: bfloat16 [32, 3072, 6144], P('rep', None, 'fsdp'), may hold values from -6 to 6
- row_state: float32 [32, 3072], P('rep'), may hold values from 3.1789146e-08 to 9.536743e-06
- col_state: float32 [32, 6144], P('rep', 'fsdp'), may hold values from 3.1789146e-08 to 9.536743e-06
- anchor: float32 [3072, 6144], P('rep', 'fsdp'), may hold values from -6 to 6
- momentum: float32 [3072, 6144], P('rep', 'fsdp'), may hold values from -4 to 4
Outputs:
- merged_weight: bfloat16 [32, 3072, 6144], P('rep', None, 'fsdp')
- row_next: float32 [32, 3072], P('rep')
- col_next: float32 [32, 6144], P('rep', 'fsdp')
- anchor_next: float32 [3072, 6144], P('rep', 'fsdp')
- momentum_next: float32 [3072, 6144], P('rep', 'fsdp')
The draws below stay inside these ranges and needn't reach their ends.
All inputs are finite; a program needn't handle non-finite values.
Results may differ from the reference program's by a relative error of at most 0.015.
Values may be sent and summed in bfloat16 or wider, within the bound.
No kernel may reach another device: no remote copies, remote signals or barrier semaphores. Data moves between devices by JAX's collectives and lax.ppermute only.
A program may use at most 128 MiB of HBM per device.

```python
import math
import jax
import jax.numpy as jnp
from jax import lax

D = 6144
HF = 3072
REPLICAS = 32
ISLAND = 1024
TOKENS = 32768


def draw_targets(key, part):
    key = jax.random.fold_in(key, 7)
    key_cols, key_vals = jax.random.split(key, 2)
    column = jnp.arange(D, dtype=jnp.float32) / D
    spread = jnp.exp(jax.random.uniform(key_cols, (D,), jnp.float32, 0.0, 1.0) * jnp.log(3.0))
    scales = jnp.exp(column * jnp.log(3.0)) * spread
    values = jax.random.uniform(key_vals, (TOKENS, D), jnp.float32, -1.7, 1.7)
    return (values * scales[None, :]).astype(jnp.bfloat16)


def raised(values, rng, source, target, shards_of, factor):
    def block_of(dim):
        return (jnp.arange(values.shape[dim]) // (values.shape[dim] // shards_of)).reshape((-1,) + (1,) * (values.ndim - 1 - dim))

    first = jax.random.permutation(rng, shards_of)[block_of(target)]
    far = (block_of(target) + shards_of // 2) % shards_of
    return jnp.where((block_of(source) == first) | (block_of(source) == far), factor * values, values)


def block_scale(key, extent, pieces, low, top_value):
    loudness, own = 1.0, jax.random.fold_in(key, 6)
    for axis_at, blocks in pieces:
        heights = jnp.exp(jax.random.uniform(jax.random.fold_in(own, axis_at), (blocks,), jnp.float32, low / len(pieces), top_value / len(pieces)))
        loudness = loudness * jnp.repeat(heights, extent[axis_at] // blocks).reshape([-1 if axis == axis_at else 1 for axis in range(len(extent))])
    return loudness


def normal_values(stream_key, shape, deviation, bound, cuts=(), held_as=jnp.bfloat16):
    entries = jax.random.normal(stream_key, shape, jnp.float32) * deviation
    if len(cuts) > 0:
        entries = block_scale(stream_key, shape, cuts, -0.22, 0.18) * entries
    return jnp.clip(entries, min=-bound, max=bound).astype(held_as)


def heavy_noise(key, extent, deviation, most, cuts, heavy, kind=jnp.bfloat16):
    drawn = deviation * jax.random.normal(key, extent, jnp.float32)
    if cuts:
        drawn = drawn * block_scale(key, extent, cuts, -0.22, 0.18)
    return jnp.clip(raised(drawn, jax.random.fold_in(key, 3), *heavy), -most, most).astype(kind)


def setup_inputs(seed: int = 0) -> dict:
    key_list = jax.random.split(jax.random.key(seed), 8)
    activations = normal_values(key_list[0], (TOKENS, HF), 1.0, 6.0, ((0, 256),))
    targets = draw_targets(jax.random.fold_in(key_list[7], 71), 0)
    replica_weight = heavy_noise(key_list[2], (REPLICAS, HF, D), 1.0, 6.0, ((0, 32), (2, 8)), (0, 1, 32, 2.75))
    row_state = jnp.clip(jnp.exp(math.log(9.5367431640625e-06) - 5.7037824 * jax.random.uniform(key_list[3], (REPLICAS, HF), jnp.float32) ** block_scale(key_list[3], (REPLICAS, HF), ((0, 32),), -0.2, 0.2)), 3.1789145538141383e-08, 9.5367431640625e-06)
    col_state = jnp.clip(jnp.exp(math.log(9.5367431640625e-06) - 5.7037824 * jax.random.uniform(key_list[4], (REPLICAS, D), jnp.float32) ** block_scale(key_list[4], (REPLICAS, D), ((0, 32), (1, 8)), -0.2, 0.2)), 3.1789145538141383e-08, 9.5367431640625e-06)
    anchor = normal_values(key_list[5], (HF, D), 1.0, 6.0, ((0, 32), (1, 8)), jnp.float32)
    momentum = normal_values(key_list[6], (HF, D), 0.5, 4.0, ((0, 32), (1, 8)), jnp.float32)
    return {"activations": activations, "targets": targets, "replica_weight": replica_weight, "row_state": row_state, "col_state": col_state, "anchor": anchor, "momentum": momentum}


decay_second = 0.95
inner_rate = 0.25
weight_decay = 0.1
outer_rate = 0.7
outer_momentum = 0.9

def replica_step(acts, goal, weight, rows, cols, anchor_half):
    inv_root = 1.0 / jnp.sqrt(jnp.float32(HF))
    output = jnp.dot(acts, weight, preferred_element_type=jnp.float32) * inv_root
    resid = (output - goal.astype(jnp.float32)).astype(jnp.bfloat16)
    grad = jnp.dot(acts.T, resid, preferred_element_type=jnp.float32) * (inv_root / ISLAND)
    squares = grad * grad + 1e-30
    row_new = decay_second * rows + (1.0 - decay_second) * (lax.optimization_barrier(jnp.sum(squares, axis=1)) / D)
    col_new = decay_second * cols + (1.0 - decay_second) * (lax.optimization_barrier(jnp.sum(squares, axis=0)) / HF)
    second = row_new[:, None] * col_new[None, :] / jnp.mean(row_new)
    wide = weight.astype(jnp.float32)
    inner = wide - inner_rate * (grad * lax.rsqrt(second) + weight_decay * wide)
    merged = (0.5 * inner + 0.5 * anchor_half.astype(jnp.float32)).astype(jnp.bfloat16)
    return (merged, row_new, col_new)

def reference(activations, targets, replica_weight, row_state, col_state, anchor, momentum):
    total = lax.optimization_barrier(jnp.sum(replica_weight, axis=0, dtype=jnp.float32))
    outer_grad = anchor - total / REPLICAS
    momentum_next = outer_momentum * momentum + outer_grad
    anchor_next = anchor - outer_rate * (outer_grad + outer_momentum * momentum_next)
    anchor_half = anchor_next.astype(jnp.bfloat16)
    acts = activations.reshape(REPLICAS, ISLAND, HF)
    goals = targets.reshape(REPLICAS, ISLAND, D)

    def one(items):
        return replica_step(items[0], items[1], items[2], items[3], items[4], anchor_half)
    merged, row_next, col_next = lax.map(one, (acts, goals, replica_weight, row_state, col_state))
    return (merged, row_next, col_next, anchor_next, momentum_next)
```

```python
import functools

import jax
import jax.numpy as jnp
from jax import lax
from jax.experimental import pallas as pl
from jax.experimental.pallas import tpu as pltpu
from jax.sharding import Mesh, PartitionSpec as P

D = 6144
decay_second = 0.95
inner_rate = 0.25
weight_decay = 0.1
outer_rate = 0.7
outer_momentum = 0.9

NZ, NX, NC, NH, NY = 4, 4, 2, 2, 4
VMEM_LIMIT = 48 * 1024 * 1024


def ring(n, k):
    return [(i, (i + k) % n) for i in range(n)]


def resid_kernel(scale, heights, index_ref, w_ref, *refs):
    n = len(heights)
    blocks, goals, out_ref = refs[:n], refs[n:-1], refs[-1]
    acts = jnp.concatenate([b[...] for b in blocks], axis=0)
    output = jnp.dot(acts, w_ref[...], preferred_element_type=jnp.float32) * scale
    goal = jnp.concatenate([g[...] for g in goals], axis=0).astype(jnp.float32)
    out_ref[...] = (output - goal).astype(jnp.bfloat16)


def resid_call(blocks, weight, targets, index, scale):
    heights = tuple(b.shape[0] for b in blocks)
    rows, hf = sum(heights), weight.shape[0]
    width, step = weight.shape[1], 256
    goals = rows // 128

    def goal_spec(i):
        return pl.BlockSpec((128, step), lambda j, s: (s[i], j))

    return pl.pallas_call(
        functools.partial(resid_kernel, scale, heights),
        grid_spec=pltpu.PrefetchScalarGridSpec(
            num_scalar_prefetch=1,
            grid=(width // step,),
            in_specs=[pl.BlockSpec((hf, step), lambda j, s: (0, j))]
            + [pl.BlockSpec(b.shape, lambda j, s: (0, 0)) for b in blocks]
            + [goal_spec(i) for i in range(goals)],
            out_specs=pl.BlockSpec((rows, step), lambda j, s: (0, j)),
        ),
        out_shape=jax.ShapeDtypeStruct((rows, width), jnp.bfloat16),
        compiler_params=pltpu.CompilerParams(vmem_limit_bytes=VMEM_LIMIT),
        cost_estimate=pl.CostEstimate(
            flops=2 * rows * hf * width,
            bytes_accessed=2 * (rows * hf + hf * width + 2 * rows * width),
            transcendentals=0,
        ),
        name="resid",
    )(index, weight, *blocks, *([targets] * goals))


def grad_kernel(scale, n, *refs):
    blocks, resids = refs[:n], refs[n:-3]
    grad_ref, row_ref, col_ref = refs[-3:]
    acts = jnp.concatenate([b[...] for b in blocks], axis=0)
    resid = jnp.concatenate([r[...] for r in resids], axis=0)
    grad = lax.dot_general(
        acts, resid, (((0,), (0,)), ((), ())), preferred_element_type=jnp.float32
    ) * scale
    grad_ref[...] = grad
    squares = grad * grad + 1e-30
    width = squares.shape[1]
    part = squares[:, :128]
    for k in range(1, width // 128):
        part = part + squares[:, k * 128 : (k + 1) * 128]
    row_ref[...] = jnp.sum(part.T, axis=0, keepdims=True)

    @pl.when(pl.program_id(0) == 0)
    def _():
        col_ref[...] = jnp.zeros_like(col_ref)

    col_ref[...] += jnp.sum(squares, axis=0, keepdims=True)


def grad_call(blocks, resids, scale):
    rows = sum(b.shape[0] for b in blocks)
    hf, width, step = blocks[0].shape[1], resids[0].shape[1], 256
    return pl.pallas_call(
        functools.partial(grad_kernel, scale, len(blocks)),
        grid=(hf // step,),
        in_specs=[pl.BlockSpec((b.shape[0], step), lambda j: (0, j)) for b in blocks]
        + [pl.BlockSpec(r.shape, lambda j: (0, 0)) for r in resids],
        out_specs=[
            pl.BlockSpec((step, width), lambda j: (j, 0)),
            pl.BlockSpec((1, step), lambda j: (0, j)),
            pl.BlockSpec((1, width), lambda j: (0, 0)),
        ],
        out_shape=[
            jax.ShapeDtypeStruct((hf, width), jnp.float32),
            jax.ShapeDtypeStruct((1, hf), jnp.float32),
            jax.ShapeDtypeStruct((1, width), jnp.float32),
        ],
        compiler_params=pltpu.CompilerParams(vmem_limit_bytes=VMEM_LIMIT),
        cost_estimate=pl.CostEstimate(
            flops=2 * rows * hf * width,
            bytes_accessed=2 * rows * (hf + width) + 4 * hf * width,
            transcendentals=0,
        ),
        name="grad",
    )(*blocks, *resids)


SLOTS = 4


def merge_kernel(pieces, index_ref, row_ref, col_ref, grad_ref, w_ref, *refs):
    n = len(pieces)
    sources, out_ref = refs[:-9], refs[-9]
    g_buf, w_buf, a_buf, o_buf, g_sem, w_sem, a_sem, o_sem = refs[-8:]
    rows = g_buf.shape[1]

    def at(i):
        return pl.ds(pl.multiple_of(index_ref[i] * rows, rows), rows)

    def loads(i):
        s = i % SLOTS
        array, part = pieces[i]
        return (
            pltpu.make_async_copy(grad_ref.at[at(i)], g_buf.at[s], g_sem.at[s]),
            pltpu.make_async_copy(w_ref.at[at(i)], w_buf.at[s], w_sem.at[s]),
            pltpu.make_async_copy(sources[array].at[part], a_buf.at[s], a_sem.at[s]),
        )

    def store(i):
        s = i % SLOTS
        return pltpu.make_async_copy(o_buf.at[s], out_ref.at[at(i)], o_sem.at[s])

    for i in range(SLOTS - 1):
        for copy in loads(i):
            copy.start()
    for i in range(n):
        if i + SLOTS - 1 < n:
            for copy in loads(i + SLOTS - 1):
                copy.start()
        for copy in loads(i):
            copy.wait()
        s = i % SLOTS
        if i >= SLOTS:
            store(i - SLOTS).wait()
        factor = row_ref[:, i : i + 1] * col_ref[...]
        w = w_buf[s].astype(jnp.float32)
        a = a_buf[s].astype(jnp.float32)
        keep = 0.5 * (1.0 - inner_rate * weight_decay)
        merged = keep * w - (0.5 * inner_rate) * (g_buf[s] * factor) + 0.5 * a
        o_buf[s] = merged.astype(jnp.bfloat16)
        store(i).start()
    for i in range(n - SLOTS, n):
        store(i).wait()


def merge_call(sources, pieces, index, rowfac, colfac, grad, weight):
    rows, width = 96, weight.shape[1]
    vmem = pl.BlockSpec(memory_space=pltpu.VMEM)
    anywhere = pl.BlockSpec(memory_space=pl.ANY)
    return pl.pallas_call(
        functools.partial(merge_kernel, pieces),
        in_specs=[pl.BlockSpec(memory_space=pltpu.SMEM), vmem, vmem, anywhere, anywhere]
        + [anywhere] * len(sources),
        out_specs=anywhere,
        out_shape=jax.ShapeDtypeStruct(weight.shape, jnp.bfloat16),
        scratch_shapes=[
            pltpu.VMEM((SLOTS, rows, width), jnp.float32),
            pltpu.VMEM((SLOTS, rows, width), jnp.bfloat16),
            pltpu.VMEM((SLOTS, rows, width), jnp.bfloat16),
            pltpu.VMEM((SLOTS, rows, width), jnp.bfloat16),
        ]
        + [pltpu.SemaphoreType.DMA((SLOTS,))] * 4,
        compiler_params=pltpu.CompilerParams(vmem_limit_bytes=VMEM_LIMIT),
        cost_estimate=pl.CostEstimate(
            flops=8 * weight.size, bytes_accessed=10 * weight.size, transcendentals=0
        ),
        name="merge",
    )(index, rowfac, colfac, grad, weight, *sources)


def body(activations, targets, replica_weight, row_state, col_state, anchor, momentum):
    weight = replica_weight[0]
    hf, width = weight.shape
    island = targets.shape[0]
    inv_root = 1.0 / float(hf) ** 0.5
    zl, x, c = lax.axis_index("zl"), lax.axis_index("x"), lax.axis_index("c")
    zh, y = lax.axis_index("zh"), lax.axis_index("y")
    rows = hf // (NZ * NX * NC)

    grid = weight.reshape(NZ, NX, NC, rows, width)
    theirs = lax.dynamic_index_in_dim(grid, 1 - c, 2, keepdims=False)
    mine = lax.dynamic_index_in_dim(grid, c, 2, keepdims=False)
    pair = lax.ppermute(theirs, "c", ring(NC, 1))
    both = (mine.astype(jnp.float32) + pair.astype(jnp.float32)).astype(jnp.bfloat16)

    def piece(k, dx):
        return lax.dynamic_slice(
            both, ((zl + k) % NZ, (x + dx) % NX, 0, 0), (1, 1, rows, width)
        ).reshape(1, rows, width)

    over_x = {}
    for ks in ((2, 1), (3, 0)):
        total = jnp.concatenate([piece(k, 0) for k in ks]).astype(jnp.float32)
        for dx in (1, 3, 2):
            sent = jnp.concatenate([piece(k, dx) for k in ks])
            total = total + lax.ppermute(sent, "x", ring(NX, dx)).astype(jnp.float32)
        for i, k in enumerate(ks):
            over_x[k] = total[i]
    share = over_x[0]
    for k in (2, 1, 3):
        share = share + lax.ppermute(
            over_x[k].astype(jnp.bfloat16), "zl", ring(NZ, k)
        ).astype(jnp.float32)

    outer_grad = anchor - share / (NZ * NX * NC)
    momentum_next = outer_momentum * momentum + outer_grad
    anchor_next = anchor - outer_rate * (outer_grad + outer_momentum * momentum_next)
    half = anchor_next.astype(jnp.bfloat16)[None]

    over_z = [lax.ppermute(half, "zl", ring(NZ, k)) for k in (1, 2, 3)]
    groups = [((0,), half), ((1, 2, 3), jnp.concatenate(over_z))]
    sources, pieces, places = [], [], []
    for ks, held in groups:
        for dx in (0, 1, 3, 2):
            got = held if dx == 0 else lax.ppermute(held, "x", ring(NX, dx))
            for swap in (0, 1):
                array = lax.ppermute(got, "c", ring(NC, 1)) if swap else got
                for i, k in enumerate(ks):
                    pieces.append((len(sources), i))
                    places.append(
                        ((zl + NZ - k) % NZ * NX + (x + NX - dx) % NX) * NC
                        + (c + swap) % NC
                    )
                sources.append(array)
    places = jnp.stack(places).astype(jnp.int32)

    def send(block, axis, k):
        return lax.ppermute(block, axis, ring(NY if axis == "y" else NH, k))

    cut = activations.shape[0] // 2
    a0, a1 = activations[:cut], activations[cut:]
    z0, z1 = send(a0, "zh", 1), send(a1, "zh", 1)
    up, down = send(activations, "y", 1), send(activations, "y", -1)
    far0, far1 = send(up[:cut], "y", 1), send(down[cut:], "y", -1)
    zup0, zdown0 = send(z0, "y", 1), send(z0, "y", -1)
    zup1, zdown1 = send(z1, "y", 1), send(z1, "y", -1)
    zfar0, zfar1 = send(zup0, "y", 1), send(zdown1, "y", -1)

    def goal(dz, dy):
        return (zh + dz) % NH * NY + (y + dy) % NY

    parts = [
        ([activations, up], [goal(0, 0), goal(0, 3)]),
        ([down, far0, far1], [goal(0, 1), goal(0, 2)]),
        ([z0, z1, zup0, zup1], [goal(1, 0), goal(1, 3)]),
        ([zdown0, zdown1, zfar0, zfar1], [goal(1, 1), goal(1, 2)]),
    ]
    resids = [
        resid_call(blocks, weight, targets, jnp.stack(goals).astype(jnp.int32), inv_root)
        for blocks, goals in parts
    ]
    grad, row_sum, col_sum = grad_call(
        [b for blocks, _ in parts for b in blocks], resids, inv_root / island
    )

    row_sum = row_sum.reshape(hf // 128, 128)
    row_total = row_sum
    for k in (1, 2, 3):
        row_total = row_total + send(row_sum, "y", k)
    row_total = row_total + send(row_total, "zh", 1)
    row_new = decay_second * row_state[0] + (1.0 - decay_second) * (
        row_total.reshape(hf) / D
    )
    col_new = decay_second * col_state + (1.0 - decay_second) * (col_sum / hf)
    rowfac = lax.rsqrt(row_new).reshape(NZ * NX * NC, rows)[places].T
    colfac = lax.rsqrt(col_new) * jnp.sqrt(jnp.mean(row_new))

    merged = merge_call(sources, tuple(pieces), places, rowfac, colfac, grad, weight)
    return (merged[None], row_new[None], col_new, anchor_next, momentum_next)


def solution(mesh):
    fine = Mesh(
        mesh.devices.reshape(NZ, NX, NC, NH, NY), ("zl", "x", "c", "zh", "y")
    )
    rep, fsdp = ("zl", "x", "c"), ("zh", "y")
    placed = (
        P(rep + fsdp, None),
        P(rep, fsdp),
        P(rep, None, fsdp),
        P(rep, None),
        P(rep, fsdp),
        P(rep, fsdp),
        P(rep, fsdp),
    )
    return jax.shard_map(
        body,
        mesh=fine,
        in_specs=placed,
        out_specs=(
            P(rep, None, fsdp),
            P(rep, None),
            P(rep, fsdp),
            P(rep, fsdp),
            P(rep, fsdp),
        ),
        check_vma=False,
    )
```

```python
import functools

import jax
import jax.numpy as jnp
from jax import lax
from jax.experimental import pallas as pl
from jax.experimental.pallas import tpu as pltpu
from jax.sharding import Mesh, PartitionSpec as P

D = 6144
decay_second = 0.95
inner_rate = 0.25
weight_decay = 0.1
outer_rate = 0.7
outer_momentum = 0.9

NZ, NX, NC, NH, NY = 4, 4, 2, 2, 4
VMEM_LIMIT = 60 * 1024 * 1024
SMALL_LIMIT = 12 * 1024 * 1024
SHADE = 16


def after(value, *others):
    return lax.optimization_barrier((value, *others))[0]


def ring(n, k):
    return [(i, (i + k) % n) for i in range(n)]


def pieces_kernel(n, index_ref, *refs):
    mine, pair, outs = refs[:n], refs[n : 2 * n], refs[2 * n :]
    for a, b, out in zip(mine, pair, outs):
        total = a[0, 0, 0].astype(jnp.float32) + b[0, 0].astype(jnp.float32)
        out[0] = total.astype(out.dtype)


def pieces_call(grid, pair, c, columns):
    nz, nx, _, rows, width = grid.shape
    n = len(columns)
    index = jnp.stack([c, *columns]).astype(jnp.int32)

    def mine_spec(i):
        return pl.BlockSpec((1, 1, 1, rows, width), lambda j, s: (j, s[i + 1], s[0], 0, 0))

    def pair_spec(i):
        return pl.BlockSpec((1, 1, rows, width), lambda j, s: (j, s[i + 1], 0, 0))

    return pl.pallas_call(
        functools.partial(pieces_kernel, n),
        grid_spec=pltpu.PrefetchScalarGridSpec(
            num_scalar_prefetch=1,
            grid=(nz,),
            in_specs=[mine_spec(i) for i in range(n)] + [pair_spec(i) for i in range(n)],
            out_specs=[pl.BlockSpec((1, rows, width), lambda j, s: (j, 0, 0))] * n,
        ),
        out_shape=[jax.ShapeDtypeStruct((nz, rows, width), jnp.bfloat16)] * n,
        compiler_params=pltpu.CompilerParams(vmem_limit_bytes=SMALL_LIMIT),
        cost_estimate=pl.CostEstimate(
            flops=0, bytes_accessed=400 * 1000 * 1000, transcendentals=0
        ),
        name="pieces",
    )(index, *([grid] * n), *([pair] * n))


def corner_kernel(in_ref, out_ref):
    out_ref[...] = in_ref[...]


def corner(array):
    block = pl.BlockSpec((16, 128), lambda i: (0, 0))
    return pl.pallas_call(
        corner_kernel,
        grid=(1,),
        in_specs=[block],
        out_specs=block,
        out_shape=jax.ShapeDtypeStruct((16, 128), array.dtype),
        compiler_params=pltpu.CompilerParams(vmem_limit_bytes=SMALL_LIMIT),
        name="corner",
    )(array)


def total_kernel(index_ref, here, near, back, far, corner_ref, a_ref, b_ref, c_ref, own_ref):
    step = pl.program_id(0)
    total = here[0].astype(jnp.float32)
    for array in (near, back, far):
        total = total + array[0].astype(jnp.float32)

    for i, out in enumerate((a_ref, b_ref, c_ref, own_ref)):

        @pl.when(step == i)
        def _(out=out):
            out[...] = total.astype(out.dtype)


def total_call(arrays, waited, order):
    nz, rows, width = arrays[0].shape
    block = pl.BlockSpec((1, rows, width), lambda j, s: (s[j], 0, 0))
    out = pl.BlockSpec((rows, width), lambda j, s: (0, 0))
    half = jax.ShapeDtypeStruct((rows, width), jnp.bfloat16)
    return pl.pallas_call(
        total_kernel,
        grid_spec=pltpu.PrefetchScalarGridSpec(
            num_scalar_prefetch=1,
            grid=(nz,),
            in_specs=[block] * 4 + [pl.BlockSpec(memory_space=pl.ANY)],
            out_specs=[out] * 4,
        ),
        out_shape=[half] * 3 + [jax.ShapeDtypeStruct((rows, width), jnp.float32)],
        compiler_params=pltpu.CompilerParams(vmem_limit_bytes=SMALL_LIMIT),
        name="total",
    )(order, *arrays, waited)


def resid_kernel(scale, heights, index_ref, w_ref, *refs):
    n = len(heights)
    blocks, goals, out_ref = refs[:n], refs[n:-1], refs[-1]
    acts = jnp.concatenate([b[...] for b in blocks], axis=0)
    output = jnp.dot(acts, w_ref[...], preferred_element_type=jnp.float32) * scale
    goal = jnp.concatenate([g[...] for g in goals], axis=0).astype(jnp.float32)
    out_ref[...] = (output - goal).astype(jnp.bfloat16)


def resid_call(blocks, weight, targets, index, scale):
    heights = tuple(b.shape[0] for b in blocks)
    rows, hf = sum(heights), weight.shape[0]
    width, step = weight.shape[1], 256
    goals = rows // 128

    def goal_spec(i):
        return pl.BlockSpec((128, step), lambda j, s: (s[i], j))

    return pl.pallas_call(
        functools.partial(resid_kernel, scale, heights),
        grid_spec=pltpu.PrefetchScalarGridSpec(
            num_scalar_prefetch=1,
            grid=(width // step,),
            in_specs=[pl.BlockSpec((hf, step), lambda j, s: (0, j))]
            + [pl.BlockSpec(b.shape, lambda j, s: (0, 0)) for b in blocks]
            + [goal_spec(i) for i in range(goals)],
            out_specs=pl.BlockSpec((rows, step), lambda j, s: (0, j)),
        ),
        out_shape=jax.ShapeDtypeStruct((rows, width), jnp.bfloat16),
        compiler_params=pltpu.CompilerParams(vmem_limit_bytes=VMEM_LIMIT),
        cost_estimate=pl.CostEstimate(
            flops=2 * rows * hf * width // SHADE,
            bytes_accessed=2 * (rows * hf + hf * width + 2 * rows * width) // SHADE,
            transcendentals=0,
        ),
        name="resid",
    )(index, weight, *blocks, *([targets] * goals))


def grad_kernel(scale, n, m, more, *refs):
    blocks, resids = refs[:n], refs[n : n + m]
    grad_ref, row_ref, col_ref = refs[-3:]
    acts = jnp.concatenate([b[...] for b in blocks], axis=0)
    resid = jnp.concatenate([r[...] for r in resids], axis=0)
    grad = lax.dot_general(
        acts, resid, (((0,), (0,)), ((), ())), preferred_element_type=jnp.float32
    ) * scale
    grad_ref[...] = grad.astype(grad_ref.dtype)
    squares = grad * grad + 1e-30
    width = squares.shape[1]
    part = squares[:, :128]
    for k in range(1, width // 128):
        part = part + squares[:, k * 128 : (k + 1) * 128]
    row_ref[...] = jnp.sum(part.T, axis=0, keepdims=True)

    @pl.when(pl.program_id(0) == 0)
    def _():
        col_ref[...] = refs[n + m][...] if more else jnp.zeros_like(col_ref)

    col_ref[...] += jnp.sum(squares, axis=0, keepdims=True)


def grad_call(blocks, resids, scale, part, parts, partial=None):
    rows = sum(b.shape[0] for b in blocks)
    hf, width, step = blocks[0].shape[1], resids[0].shape[1], 512
    steps = hf // step // parts
    base = part * steps
    given, given_specs, aliases = [], [], {}
    if partial is not None:
        grad, row, col = partial
        given = [col, grad, row]
        given_specs = [pl.BlockSpec((1, width), lambda j: (0, 0))]
        given_specs += [pl.BlockSpec(memory_space=pl.ANY)] * 2
        first = len(blocks) + len(resids)
        aliases = {first + 1: 0, first + 2: 1}
    return pl.pallas_call(
        functools.partial(grad_kernel, scale, len(blocks), len(resids), bool(given)),
        grid=(steps,),
        in_specs=[pl.BlockSpec((b.shape[0], step), lambda j: (0, j + base)) for b in blocks]
        + [pl.BlockSpec(r.shape, lambda j: (0, 0)) for r in resids]
        + given_specs,
        out_specs=[
            pl.BlockSpec((step, width), lambda j: (j + base, 0)),
            pl.BlockSpec((1, step), lambda j: (0, j + base)),
            pl.BlockSpec((1, width), lambda j: (0, 0)),
        ],
        out_shape=[
            jax.ShapeDtypeStruct((hf, width), jnp.bfloat16),
            jax.ShapeDtypeStruct((1, hf), jnp.float32),
            jax.ShapeDtypeStruct((1, width), jnp.float32),
        ],
        input_output_aliases=aliases,
        compiler_params=pltpu.CompilerParams(vmem_limit_bytes=VMEM_LIMIT),
        cost_estimate=pl.CostEstimate(
            flops=2 * rows * hf * width // parts,
            bytes_accessed=(2 * rows * (hf + width) + 2 * hf * width) // parts,
            transcendentals=0,
        ),
        name="grad",
    )(*blocks, *resids, *given)


SLOTS = 8


def merge_kernel(
    pieces, index_ref, row_state, row_a, row_b, col_state, col_sum, grad_ref, w_ref, *refs
):
    n = len(pieces)
    sources, refs = refs[:-12], refs[-12:]
    out_ref, row_next, col_next, g_buf, w_buf, a_buf, o_buf, column = refs[:8]
    g_sem, w_sem, a_sem, o_sem = refs[8:]
    rows = w_buf.shape[1]

    def at(i):
        return pl.ds(pl.multiple_of(index_ref[i] * rows, rows), rows)

    def loads(i):
        s = i % SLOTS
        array, part = pieces[i]
        return (
            pltpu.make_async_copy(grad_ref.at[at(i)], g_buf.at[s], g_sem.at[s]),
            pltpu.make_async_copy(w_ref.at[at(i)], w_buf.at[s], w_sem.at[s]),
            pltpu.make_async_copy(sources[array].at[part], a_buf.at[s], a_sem.at[s]),
        )

    def store(i):
        s = i % SLOTS
        return pltpu.make_async_copy(o_buf.at[s], out_ref.at[at(i)], o_sem.at[s])

    for i in range(SLOTS - 1):
        for copy in loads(i):
            copy.start()

    hf = w_ref.shape[0]
    row_new = decay_second * row_state[...] + (1.0 - decay_second) * (
        (row_a[...] + row_b[...]) / D
    )
    row_next[...] = row_new
    col_new = decay_second * col_state[...] + (1.0 - decay_second) * (col_sum[...] / hf)
    col_next[...] = col_new
    turned = lax.rsqrt(row_new).T
    for i in range(turned.shape[1]):
        column[i * 128 : (i + 1) * 128, :] = turned[:, i : i + 1]
    colfac = (0.5 * inner_rate) * lax.rsqrt(col_new) * jnp.sqrt(jnp.mean(row_new))

    for i in range(n):
        if i + SLOTS - 1 < n:
            for copy in loads(i + SLOTS - 1):
                copy.start()
        for copy in loads(i):
            copy.wait()
        s = i % SLOTS
        if i >= SLOTS:
            store(i - SLOTS).wait()
        w = w_buf[s].astype(jnp.float32)
        a = a_buf[s].astype(jnp.float32)
        keep = 0.5 * (1.0 - inner_rate * weight_decay)
        step = g_buf[s].astype(jnp.float32) * column[at(i), :] * colfac
        o_buf[s] = (keep * w - step + 0.5 * a).astype(jnp.bfloat16)
        store(i).start()
    for i in range(n - SLOTS, n):
        store(i).wait()


def merge_call(sources, pieces, index, row_state, row_a, row_b, col_state, col_sum, grad, weight):
    rows, width = 96, weight.shape[1]
    vmem = pl.BlockSpec(memory_space=pltpu.VMEM)
    anywhere = pl.BlockSpec(memory_space=pl.ANY)
    return pl.pallas_call(
        functools.partial(merge_kernel, pieces),
        in_specs=[pl.BlockSpec(memory_space=pltpu.SMEM)]
        + [vmem] * 5
        + [anywhere] * (2 + len(sources)),
        out_specs=[anywhere, vmem, vmem],
        out_shape=[
            jax.ShapeDtypeStruct(weight.shape, jnp.bfloat16),
            jax.ShapeDtypeStruct(row_state.shape, jnp.float32),
            jax.ShapeDtypeStruct(col_state.shape, jnp.float32),
        ],
        scratch_shapes=[pltpu.VMEM((SLOTS, rows, width), jnp.bfloat16)] * 4
        + [pltpu.VMEM((weight.shape[0], 1), jnp.float32)]
        + [pltpu.SemaphoreType.DMA((SLOTS,))] * 4,
        compiler_params=pltpu.CompilerParams(vmem_limit_bytes=VMEM_LIMIT),
        cost_estimate=pl.CostEstimate(
            flops=8 * weight.size, bytes_accessed=8 * weight.size, transcendentals=0
        ),
        name="merge",
    )(index, row_state, row_a, row_b, col_state, col_sum, grad, weight, *sources)


def body(activations, targets, replica_weight, row_state, col_state, anchor, momentum):
    weight = replica_weight[0]
    hf, width = weight.shape
    island = targets.shape[0]
    inv_root = 1.0 / float(hf) ** 0.5
    mesh_size = {"zl": NZ, "x": NX, "c": NC, "zh": NH, "y": NY}
    zl, x, c = lax.axis_index("zl"), lax.axis_index("x"), lax.axis_index("c")
    zh, y = lax.axis_index("zh"), lax.axis_index("y")
    rows = hf // (NZ * NX * NC)

    def send(block, axis, k, what):
        with jax.named_scope(what):
            return lax.ppermute(block, axis, ring(mesh_size[axis], k))

    side = 1 - 2 * c

    def turn(block, axis, k, what):
        n = mesh_size[axis]
        axes = ("x", "c") if axis == "x" else ("c", axis)

        def place(i, j):
            return i * NC + j if axis == "x" else j * n + i

        pairs = [
            (place(i, j), place((i + (k if j == 0 else -k)) % n, j))
            for i in range(n)
            for j in range(NC)
        ]
        with jax.named_scope(what):
            return lax.ppermute(block, axes, pairs)

    grid = weight.reshape(NZ, NX, NC, rows, width)
    theirs = lax.dynamic_index_in_dim(grid, 1 - c, 2, keepdims=False)
    pair = send(theirs, "c", 1, "sum_core")
    near = turn(activations, "y", 1, "acts_near")
    zown = send(activations, "zh", 1, "acts_zown")

    half_type = jnp.bfloat16
    here, ahead, behind, across = pieces_call(
        grid, pair, c, [(x + dx + NX) % NX for dx in (0, side, -side, 2)]
    )
    far = turn(after(near, ahead), "y", 1, "acts_far")
    got_near = turn(ahead, "x", 1, "sum_near")
    got_back = turn(behind, "x", -1, "sum_back")
    got_far = send(across, "x", 2, "sum_far")
    back = turn(after(activations, got_far), "y", -1, "acts_back")
    z_order = (2, 1, 3, 0)
    *z_sent, share = total_call(
        (here, got_near, got_back, got_far),
        corner(zown),
        jnp.stack([(zl + k) % NZ for k in z_order]).astype(jnp.int32),
    )
    z_sent = [after(p, far, back) for p in z_sent]
    z_got = [send(p, "zl", k, "sum_z%d" % k) for p, k in zip(z_sent, z_order)]
    znear = turn(after(zown, *z_sent), "y", 1, "acts_znear")
    zback = turn(after(zown, *z_sent), "y", -1, "acts_zback")
    def goal(dz, dy):
        return (zh + dz) % NH * NY + (y + dy + NY) % NY

    parts = [
        (
            [activations, near, back, far],
            [goal(0, 0), goal(0, -side), goal(0, side), goal(0, 2)],
        ),
        (
            [zown, znear, zback],
            [goal(1, 0), goal(1, -side), goal(1, side), goal(1, 2)],
        ),
    ]
    def resid_of(g, *wait):
        held, goals = parts[g]
        index = after(jnp.stack(goals).astype(jnp.int32), *wait)
        return resid_call(held, weight, targets, index, inv_root)

    resids = [resid_of(0, *z_sent)]
    zfar = turn(after(znear, resids[0], *z_got), "y", 1, "acts_zfar")
    parts[1][0].append(zfar)
    for got in z_got:
        share = share + got.astype(jnp.float32)
    share = after(share, znear, zback, resids[0])

    outer_grad = anchor - share / (NZ * NX * NC)
    momentum_next = outer_momentum * momentum + outer_grad
    anchor_next = anchor - outer_rate * (outer_grad + outer_momentum * momentum_next)
    half = anchor_next.astype(jnp.bfloat16)[None]

    over_z = [send(half, "zl", k, "new_z%d" % k) for k in (1, 2, 3)]
    resids.append(resid_of(1, half))
    over_z = [after(o, *resids) for o in over_z]
    held = jnp.concatenate([half] + over_z)
    new_near = turn(held, "x", 1, "new_near")
    new_back = turn(held, "x", -1, "new_back")
    blocks = [b for blocks, _ in parts for b in blocks]
    scale = inv_root / island
    grad, row_sum, col_sum = grad_call(blocks, resids, scale, 0, 1)
    row_sum = row_sum.reshape(hf // 128, 128)
    row_a = row_sum
    for k in (1, 2, 3):
        row_a = row_a + send(row_sum, "y", k, "row_y")
    row_b = send(row_a, "zh", 1, "row_z")

    new_far = turn(after(new_near, new_back, row_a), "x", 1, "new_far")
    sources, pieces, places = [], [], []
    late = ((held, 0), (new_near, -side), (new_back, side), (new_far, 2))
    for i, (block, origin) in enumerate(late):
        for swap in (0, 1):
            from_c = 1 - c if swap else c
            from_x = (x + (-origin if swap else origin) + NX) % NX
            for k in range(NZ):
                pieces.append((len(sources), k))
                places.append(((zl + NZ - k) % NZ * NX + from_x) * NC + from_c)
            sources.append(send(after(block, row_b if i == 3 else row_a), "c", 1, "new_core") if swap else block)
    places = jnp.stack(places).astype(jnp.int32)

    merged, row_new, col_new = merge_call(
        sources,
        tuple(pieces),
        places,
        row_state.reshape(row_sum.shape),
        row_a,
        row_b,
        col_state,
        col_sum,
        grad,
        weight,
    )
    return (merged[None], row_new.reshape(row_state.shape), col_new, anchor_next, momentum_next)


def solution(mesh):
    fine = Mesh(
        mesh.devices.reshape(NZ, NX, NC, NH, NY), ("zl", "x", "c", "zh", "y")
    )
    rep, fsdp = ("zl", "x", "c"), ("zh", "y")
    placed = (
        P(rep + fsdp, None),
        P(rep, fsdp),
        P(rep, None, fsdp),
        P(rep, None),
        P(rep, fsdp),
        P(rep, fsdp),
        P(rep, fsdp),
    )
    return jax.shard_map(
        body,
        mesh=fine,
        in_specs=placed,
        out_specs=(
            P(rep, None, fsdp),
            P(rep, None),
            P(rep, fsdp),
            P(rep, fsdp),
            P(rep, fsdp),
        ),
        check_vma=False,
    )
```

```python
import functools

import jax
import jax.numpy as jnp
from jax import lax
from jax.experimental import pallas as pl
from jax.experimental.pallas import tpu as pltpu
from jax.sharding import Mesh, PartitionSpec as P

D = 6144
decay_second = 0.95
inner_rate = 0.25
weight_decay = 0.1
outer_rate = 0.7
outer_momentum = 0.9

NZ, NX, NC, NH, NY = 4, 4, 2, 2, 4
VMEM_LIMIT = 60 * 1024 * 1024
SMALL_LIMIT = 12 * 1024 * 1024
SHADE = 16


def after(value, *others):
    return lax.optimization_barrier((value, *others))[0]


def ring(n, k):
    return [(i, (i + k) % n) for i in range(n)]


def pieces_kernel(n, index_ref, *refs):
    mine, pair, outs = refs[:n], refs[n : 2 * n], refs[2 * n :]
    for a, b, out in zip(mine, pair, outs):
        total = a[0, 0, 0].astype(jnp.float32) + b[0, 0].astype(jnp.float32)
        out[0] = total.astype(out.dtype)


def pieces_call(grid, pair, c, columns):
    nz, nx, _, rows, width = grid.shape
    n = len(columns)
    index = jnp.stack([c, *columns]).astype(jnp.int32)

    def mine_spec(i):
        return pl.BlockSpec((1, 1, 1, rows, width), lambda j, s: (j, s[i + 1], s[0], 0, 0))

    def pair_spec(i):
        return pl.BlockSpec((1, 1, rows, width), lambda j, s: (j, s[i + 1], 0, 0))

    return pl.pallas_call(
        functools.partial(pieces_kernel, n),
        grid_spec=pltpu.PrefetchScalarGridSpec(
            num_scalar_prefetch=1,
            grid=(nz,),
            in_specs=[mine_spec(i) for i in range(n)] + [pair_spec(i) for i in range(n)],
            out_specs=[pl.BlockSpec((1, rows, width), lambda j, s: (j, 0, 0))] * n,
        ),
        out_shape=[jax.ShapeDtypeStruct((nz, rows, width), jnp.bfloat16)] * n,
        compiler_params=pltpu.CompilerParams(vmem_limit_bytes=SMALL_LIMIT),
        cost_estimate=pl.CostEstimate(
            flops=0, bytes_accessed=400 * 1000 * 1000, transcendentals=0
        ),
        name="pieces",
    )(index, *([grid] * n), *([pair] * n))


def corner_kernel(in_ref, waited_ref, out_ref):
    out_ref[...] = in_ref[...]


def corner(array, waited):
    block = pl.BlockSpec((16, 128), lambda i: (0, 0))
    return pl.pallas_call(
        corner_kernel,
        grid=(1,),
        in_specs=[block, pl.BlockSpec(memory_space=pl.ANY)],
        out_specs=block,
        out_shape=jax.ShapeDtypeStruct((16, 128), array.dtype),
        compiler_params=pltpu.CompilerParams(vmem_limit_bytes=SMALL_LIMIT),
        name="corner",
    )(array, waited)


def total_kernel(index_ref, here, near, back, far, *refs):
    a_ref, b_ref, c_ref, own_ref = refs[-4:]
    step = pl.program_id(0)
    total = here[0].astype(jnp.float32)
    for array in (near, back, far):
        total = total + array[0].astype(jnp.float32)

    for i, out in enumerate((a_ref, b_ref, c_ref, own_ref)):

        @pl.when(step == i)
        def _(out=out):
            out[...] = total.astype(out.dtype)


def total_call(arrays, waited, order):
    nz, rows, width = arrays[0].shape
    block = pl.BlockSpec((1, rows, width), lambda j, s: (s[j], 0, 0))
    out = pl.BlockSpec((rows, width), lambda j, s: (0, 0))
    half = jax.ShapeDtypeStruct((rows, width), jnp.bfloat16)
    return pl.pallas_call(
        total_kernel,
        grid_spec=pltpu.PrefetchScalarGridSpec(
            num_scalar_prefetch=1,
            grid=(nz,),
            in_specs=[block] * 4 + [pl.BlockSpec(memory_space=pl.ANY)] * len(waited),
            out_specs=[out] * 4,
        ),
        out_shape=[half] * 3 + [jax.ShapeDtypeStruct((rows, width), jnp.float32)],
        compiler_params=pltpu.CompilerParams(vmem_limit_bytes=SMALL_LIMIT),
        name="total",
    )(order, *arrays, *waited)


def resid_kernel(scale, heights, index_ref, w_ref, *refs):
    n = len(heights)
    blocks, goals, out_ref = refs[:n], refs[n:-1], refs[-1]
    acts = jnp.concatenate([b[...] for b in blocks], axis=0)
    output = jnp.dot(acts, w_ref[...], preferred_element_type=jnp.float32) * scale
    goal = jnp.concatenate([g[...] for g in goals], axis=0).astype(jnp.float32)
    out_ref[...] = (output - goal).astype(jnp.bfloat16)


def resid_call(blocks, weight, targets, index, scale):
    heights = tuple(b.shape[0] for b in blocks)
    rows, hf = sum(heights), weight.shape[0]
    width, step = weight.shape[1], 256
    goals = rows // 128

    def goal_spec(i):
        return pl.BlockSpec((128, step), lambda j, s: (s[i], j))

    return pl.pallas_call(
        functools.partial(resid_kernel, scale, heights),
        grid_spec=pltpu.PrefetchScalarGridSpec(
            num_scalar_prefetch=1,
            grid=(width // step,),
            in_specs=[pl.BlockSpec((hf, step), lambda j, s: (0, j))]
            + [pl.BlockSpec(b.shape, lambda j, s: (0, 0)) for b in blocks]
            + [goal_spec(i) for i in range(goals)],
            out_specs=pl.BlockSpec((rows, step), lambda j, s: (0, j)),
        ),
        out_shape=jax.ShapeDtypeStruct((rows, width), jnp.bfloat16),
        compiler_params=pltpu.CompilerParams(vmem_limit_bytes=VMEM_LIMIT),
        cost_estimate=pl.CostEstimate(
            flops=2 * rows * hf * width // SHADE,
            bytes_accessed=2 * (rows * hf + hf * width + 2 * rows * width) // SHADE,
            transcendentals=0,
        ),
        name="resid",
    )(index, weight, *blocks, *([targets] * goals))


def grad_kernel(scale, n, m, more, *refs):
    blocks, resids = refs[:n], refs[n : n + m]
    grad_ref, row_ref, col_ref = refs[-3:]
    acts = jnp.concatenate([b[...] for b in blocks], axis=0)
    resid = jnp.concatenate([r[...] for r in resids], axis=0)
    grad = lax.dot_general(
        acts, resid, (((0,), (0,)), ((), ())), preferred_element_type=jnp.float32
    ) * scale
    grad_ref[...] = grad.astype(grad_ref.dtype)
    squares = grad * grad + 1e-30
    width = squares.shape[1]
    part = squares[:, :128]
    for k in range(1, width // 128):
        part = part + squares[:, k * 128 : (k + 1) * 128]
    row_ref[...] = jnp.sum(part.T, axis=0, keepdims=True)

    @pl.when(pl.program_id(0) == 0)
    def _():
        col_ref[...] = refs[n + m][...] if more else jnp.zeros_like(col_ref)

    col_ref[...] += jnp.sum(squares, axis=0, keepdims=True)


def grad_call(blocks, resids, scale, part, parts, partial=None):
    rows = sum(b.shape[0] for b in blocks)
    hf, width, step = blocks[0].shape[1], resids[0].shape[1], 1024
    steps = hf // step // parts
    base = part * steps
    given, given_specs, aliases = [], [], {}
    if partial is not None:
        grad, row, col = partial
        given = [col, grad, row]
        given_specs = [pl.BlockSpec((1, width), lambda j: (0, 0))]
        given_specs += [pl.BlockSpec(memory_space=pl.ANY)] * 2
        first = len(blocks) + len(resids)
        aliases = {first + 1: 0, first + 2: 1}
    return pl.pallas_call(
        functools.partial(grad_kernel, scale, len(blocks), len(resids), bool(given)),
        grid=(steps,),
        in_specs=[pl.BlockSpec((b.shape[0], step), lambda j: (0, j + base)) for b in blocks]
        + [pl.BlockSpec(r.shape, lambda j: (0, 0)) for r in resids]
        + given_specs,
        out_specs=[
            pl.BlockSpec((step, width), lambda j: (j + base, 0)),
            pl.BlockSpec((1, step), lambda j: (0, j + base)),
            pl.BlockSpec((1, width), lambda j: (0, 0)),
        ],
        out_shape=[
            jax.ShapeDtypeStruct((hf, width), jnp.bfloat16),
            jax.ShapeDtypeStruct((1, hf), jnp.float32),
            jax.ShapeDtypeStruct((1, width), jnp.float32),
        ],
        input_output_aliases=aliases,
        compiler_params=pltpu.CompilerParams(vmem_limit_bytes=VMEM_LIMIT),
        cost_estimate=pl.CostEstimate(
            flops=2 * rows * hf * width // parts,
            bytes_accessed=(2 * rows * (hf + width) + 2 * hf * width) // parts,
            transcendentals=0,
        ),
        name="grad",
    )(*blocks, *resids, *given)


SLOTS = 8


def merge_kernel(
    pieces, index_ref, row_state, row_a, row_b, col_state, col_sum, grad_ref, w_ref, *refs
):
    n = len(pieces)
    sources, refs = refs[:-12], refs[-12:]
    out_ref, row_next, col_next, g_buf, w_buf, a_buf, o_buf, column = refs[:8]
    g_sem, w_sem, a_sem, o_sem = refs[8:]
    rows = w_buf.shape[1]

    def at(i):
        return pl.ds(pl.multiple_of(index_ref[i] * rows, rows), rows)

    def loads(i):
        s = i % SLOTS
        array, part = pieces[i]
        return (
            pltpu.make_async_copy(grad_ref.at[at(i)], g_buf.at[s], g_sem.at[s]),
            pltpu.make_async_copy(w_ref.at[at(i)], w_buf.at[s], w_sem.at[s]),
            pltpu.make_async_copy(sources[array].at[part], a_buf.at[s], a_sem.at[s]),
        )

    def store(i):
        s = i % SLOTS
        return pltpu.make_async_copy(o_buf.at[s], out_ref.at[at(i)], o_sem.at[s])

    for i in range(SLOTS - 1):
        for copy in loads(i):
            copy.start()

    hf = w_ref.shape[0]
    row_new = decay_second * row_state[...] + (1.0 - decay_second) * (
        (row_a[...] + row_b[...]) / D
    )
    row_next[...] = row_new
    col_new = decay_second * col_state[...] + (1.0 - decay_second) * (col_sum[...] / hf)
    col_next[...] = col_new
    turned = lax.rsqrt(row_new).T
    for i in range(turned.shape[1]):
        column[i * 128 : (i + 1) * 128, :] = turned[:, i : i + 1]
    colfac = (0.5 * inner_rate) * lax.rsqrt(col_new) * jnp.sqrt(jnp.mean(row_new))

    for i in range(n):
        if i + SLOTS - 1 < n:
            for copy in loads(i + SLOTS - 1):
                copy.start()
        for copy in loads(i):
            copy.wait()
        s = i % SLOTS
        if i >= SLOTS:
            store(i - SLOTS).wait()
        w = w_buf[s].astype(jnp.float32)
        a = a_buf[s].astype(jnp.float32)
        keep = 0.5 * (1.0 - inner_rate * weight_decay)
        step = g_buf[s].astype(jnp.float32) * column[at(i), :] * colfac
        o_buf[s] = (keep * w - step + 0.5 * a).astype(jnp.bfloat16)
        store(i).start()
    for i in range(n - SLOTS, n):
        store(i).wait()


def merge_call(sources, pieces, index, row_state, row_a, row_b, col_state, col_sum, grad, weight):
    rows, width = 96, weight.shape[1]
    vmem = pl.BlockSpec(memory_space=pltpu.VMEM)
    anywhere = pl.BlockSpec(memory_space=pl.ANY)
    return pl.pallas_call(
        functools.partial(merge_kernel, pieces),
        in_specs=[pl.BlockSpec(memory_space=pltpu.SMEM)]
        + [vmem] * 5
        + [anywhere] * (2 + len(sources)),
        out_specs=[anywhere, vmem, vmem],
        out_shape=[
            jax.ShapeDtypeStruct(weight.shape, jnp.bfloat16),
            jax.ShapeDtypeStruct(row_state.shape, jnp.float32),
            jax.ShapeDtypeStruct(col_state.shape, jnp.float32),
        ],
        scratch_shapes=[pltpu.VMEM((SLOTS, rows, width), jnp.bfloat16)] * 4
        + [pltpu.VMEM((weight.shape[0], 1), jnp.float32)]
        + [pltpu.SemaphoreType.DMA((SLOTS,))] * 4,
        compiler_params=pltpu.CompilerParams(vmem_limit_bytes=VMEM_LIMIT),
        cost_estimate=pl.CostEstimate(
            flops=8 * weight.size, bytes_accessed=8 * weight.size, transcendentals=0
        ),
        name="merge",
    )(index, row_state, row_a, row_b, col_state, col_sum, grad, weight, *sources)


def body(activations, targets, replica_weight, row_state, col_state, anchor, momentum):
    weight = replica_weight[0]
    hf, width = weight.shape
    island = targets.shape[0]
    inv_root = 1.0 / float(hf) ** 0.5
    mesh_size = {"zl": NZ, "x": NX, "c": NC, "zh": NH, "y": NY}
    zl, x, c = lax.axis_index("zl"), lax.axis_index("x"), lax.axis_index("c")
    zh, y = lax.axis_index("zh"), lax.axis_index("y")
    rows = hf // (NZ * NX * NC)

    def send(block, axis, k, what):
        with jax.named_scope(what):
            return lax.ppermute(block, axis, ring(mesh_size[axis], k))

    side = 1 - 2 * c

    def turn(block, axis, k, what):
        n = mesh_size[axis]
        axes = ("x", "c") if axis == "x" else ("c", axis)

        def place(i, j):
            return i * NC + j if axis == "x" else j * n + i

        pairs = [
            (place(i, j), place((i + (k if j == 0 else -k)) % n, j))
            for i in range(n)
            for j in range(NC)
        ]
        with jax.named_scope(what):
            return lax.ppermute(block, axes, pairs)

    grid = weight.reshape(NZ, NX, NC, rows, width)
    theirs = lax.dynamic_index_in_dim(grid, 1 - c, 2, keepdims=False)
    pair = send(theirs, "c", 1, "sum_core")
    near = turn(activations, "y", 1, "acts_near")
    zown = send(activations, "zh", 1, "acts_zown")

    half_type = jnp.bfloat16
    here, ahead, behind, across = pieces_call(
        grid, pair, c, [(x + dx + NX) % NX for dx in (0, side, -side, 2)]
    )
    far = turn(after(near, ahead), "y", 1, "acts_far")
    got_near = turn(ahead, "x", 1, "sum_near")
    got_back = turn(behind, "x", -1, "sum_back")
    got_far = send(across, "x", 2, "sum_far")
    back = turn(after(activations, far), "y", -1, "acts_back")
    def goal(dz, dy):
        return (zh + dz) % NH * NY + (y + dy + NY) % NY

    parts = [
        (
            [activations, near],
            [goal(0, 0), goal(0, -side)],
        ),
        (
            [far],
            [goal(0, 2), goal(1, 0), goal(1, -side), goal(1, side)],
        ),
        (
            [back],
            [goal(0, side), goal(1, 2)],
        ),
    ]
    def resid_of(g, *wait):
        held, goals = parts[g]
        index = after(jnp.stack(goals).astype(jnp.int32), *wait)
        return resid_call(held, weight, targets, index, inv_root)

    resids = [resid_of(0)]
    z_order = (2, 1, 3, 0)
    *z_sent, share = total_call(
        (here, got_near, got_back, got_far),
        (corner(zown, resids[0]),),
        jnp.stack([(zl + k) % NZ for k in z_order]).astype(jnp.int32),
    )
    z_sent = [after(p, far) for p in z_sent]
    z_got = [send(p, "zl", k, "sum_z%d" % k) for p, k in zip(z_sent, z_order)]
    znear = turn(after(zown, *z_sent), "y", 1, "acts_znear")
    zback = turn(after(zown, *z_sent), "y", -1, "acts_zback")
    zfar = turn(after(znear, *z_got), "y", 1, "acts_zfar")
    for got in z_got:
        share = share + got.astype(jnp.float32)
    parts[1][0].extend((zown, znear, zback))
    parts[2][0].append(zfar)
    share = after(share, znear)

    outer_grad = anchor - share / (NZ * NX * NC)
    momentum_next = outer_momentum * momentum + outer_grad
    anchor_next = anchor - outer_rate * (outer_grad + outer_momentum * momentum_next)
    half = anchor_next.astype(jnp.bfloat16)[None]

    over_z = [send(half, "zl", k, "new_z%d" % k) for k in (1, 2, 3)]
    resids += [resid_of(1, half), resid_of(2, half)]
    over_z = [after(o, *resids[:2]) for o in over_z]
    held = jnp.concatenate([half] + over_z)
    new_near = turn(held, "x", 1, "new_near")
    new_back = turn(held, "x", -1, "new_back")
    blocks = [b for blocks, _ in parts for b in blocks]
    scale = inv_root / island
    grad, row_sum, col_sum = grad_call(blocks, resids, scale, 0, 1)
    row_sum = row_sum.reshape(hf // 128, 128)
    row_a = row_sum
    for k in (1, 2, 3):
        row_a = row_a + send(row_sum, "y", k, "row_y")
    row_b = send(row_a, "zh", 1, "row_z")

    new_far = turn(after(new_near, new_back, row_sum), "x", 1, "new_far")
    sources, pieces, places = [], [], []
    late = ((held, 0), (new_near, -side), (new_back, side), (new_far, 2))
    for i, (block, origin) in enumerate(late):
        for swap in (0, 1):
            from_c = 1 - c if swap else c
            from_x = (x + (-origin if swap else origin) + NX) % NX
            for k in range(NZ):
                pieces.append((len(sources), k))
                places.append(((zl + NZ - k) % NZ * NX + from_x) * NC + from_c)
            sources.append(send(after(block, row_b if i == 3 else row_a), "c", 1, "new_core") if swap else block)
    places = jnp.stack(places).astype(jnp.int32)

    merged, row_new, col_new = merge_call(
        sources,
        tuple(pieces),
        places,
        row_state.reshape(row_sum.shape),
        row_a,
        row_b,
        col_state,
        col_sum,
        grad,
        weight,
    )
    return (merged[None], row_new.reshape(row_state.shape), col_new, anchor_next, momentum_next)


def solution(mesh):
    fine = Mesh(
        mesh.devices.reshape(NZ, NX, NC, NH, NY), ("zl", "x", "c", "zh", "y")
    )
    rep, fsdp = ("zl", "x", "c"), ("zh", "y")
    placed = (
        P(rep + fsdp, None),
        P(rep, fsdp),
        P(rep, None, fsdp),
        P(rep, None),
        P(rep, fsdp),
        P(rep, fsdp),
        P(rep, fsdp),
    )
    return jax.shard_map(
        body,
        mesh=fine,
        in_specs=placed,
        out_specs=(
            P(rep, None, fsdp),
            P(rep, None),
            P(rep, fsdp),
            P(rep, fsdp),
            P(rep, fsdp),
        ),
        check_vma=False,
    )
```

```python
import functools

import jax
import jax.numpy as jnp
from jax import lax
from jax.experimental import pallas as pl
from jax.experimental.pallas import tpu as pltpu
from jax.sharding import Mesh, PartitionSpec as P

D = 6144
decay_second = 0.95
inner_rate = 0.25
weight_decay = 0.1
outer_rate = 0.7
outer_momentum = 0.9

NZ, NX, NC, NH, NY = 4, 4, 2, 2, 4
VMEM_LIMIT = 60 * 1024 * 1024
SMALL_LIMIT = 12 * 1024 * 1024
SHADE = 16


def after(value, *others):
    return lax.optimization_barrier((value, *others))[0]


def ring(n, k):
    return [(i, (i + k) % n) for i in range(n)]


def pieces_kernel(n, index_ref, *refs):
    mine, pair, outs = refs[:n], refs[n : 2 * n], refs[2 * n :]
    for a, b, out in zip(mine, pair, outs):
        total = a[0, 0, 0].astype(jnp.float32) + b[0, 0].astype(jnp.float32)
        out[0] = total.astype(out.dtype)


def pieces_call(grid, pair, c, columns):
    nz, nx, _, rows, width = grid.shape
    n = len(columns)
    index = jnp.stack([c, *columns]).astype(jnp.int32)

    def mine_spec(i):
        return pl.BlockSpec((1, 1, 1, rows, width), lambda j, s: (j, s[i + 1], s[0], 0, 0))

    def pair_spec(i):
        return pl.BlockSpec((1, 1, rows, width), lambda j, s: (j, s[i + 1], 0, 0))

    return pl.pallas_call(
        functools.partial(pieces_kernel, n),
        grid_spec=pltpu.PrefetchScalarGridSpec(
            num_scalar_prefetch=1,
            grid=(nz,),
            in_specs=[mine_spec(i) for i in range(n)] + [pair_spec(i) for i in range(n)],
            out_specs=[pl.BlockSpec((1, rows, width), lambda j, s: (j, 0, 0))] * n,
        ),
        out_shape=[jax.ShapeDtypeStruct((nz, rows, width), jnp.bfloat16)] * n,
        compiler_params=pltpu.CompilerParams(vmem_limit_bytes=SMALL_LIMIT),
        cost_estimate=pl.CostEstimate(
            flops=0, bytes_accessed=400 * 1000 * 1000, transcendentals=0
        ),
        name="pieces",
    )(index, *([grid] * n), *([pair] * n))


def corner_kernel(in_ref, waited_ref, out_ref):
    out_ref[...] = in_ref[...]


def corner(array, waited):
    block = pl.BlockSpec((16, 128), lambda i: (0, 0))
    return pl.pallas_call(
        corner_kernel,
        grid=(1,),
        in_specs=[block, pl.BlockSpec(memory_space=pl.ANY)],
        out_specs=block,
        out_shape=jax.ShapeDtypeStruct((16, 128), array.dtype),
        compiler_params=pltpu.CompilerParams(vmem_limit_bytes=SMALL_LIMIT),
        name="corner",
    )(array, waited)


def total_kernel(index_ref, here, near, back, far, *refs):
    a_ref, b_ref, c_ref, own_ref = refs[-4:]
    step = pl.program_id(0)
    total = here[0].astype(jnp.float32)
    for array in (near, back, far):
        total = total + array[0].astype(jnp.float32)

    for i, out in enumerate((a_ref, b_ref, c_ref, own_ref)):

        @pl.when(step == i)
        def _(out=out):
            out[...] = total.astype(out.dtype)


def total_call(arrays, waited, order):
    nz, rows, width = arrays[0].shape
    block = pl.BlockSpec((1, rows, width), lambda j, s: (s[j], 0, 0))
    out = pl.BlockSpec((rows, width), lambda j, s: (0, 0))
    half = jax.ShapeDtypeStruct((rows, width), jnp.bfloat16)
    return pl.pallas_call(
        total_kernel,
        grid_spec=pltpu.PrefetchScalarGridSpec(
            num_scalar_prefetch=1,
            grid=(nz,),
            in_specs=[block] * 4 + [pl.BlockSpec(memory_space=pl.ANY)] * len(waited),
            out_specs=[out] * 4,
        ),
        out_shape=[half] * 3 + [jax.ShapeDtypeStruct((rows, width), jnp.float32)],
        compiler_params=pltpu.CompilerParams(vmem_limit_bytes=SMALL_LIMIT),
        name="total",
    )(order, *arrays, *waited)


def resid_kernel(scale, heights, index_ref, w_ref, *refs):
    n = len(heights)
    blocks, goals, out_ref = refs[:n], refs[n:-1], refs[-1]
    acts = jnp.concatenate([b[...] for b in blocks], axis=0)
    output = jnp.dot(acts, w_ref[...], preferred_element_type=jnp.float32) * scale
    goal = jnp.concatenate([g[...] for g in goals], axis=0).astype(jnp.float32)
    out_ref[...] = (output - goal).astype(jnp.bfloat16)


def resid_call(blocks, weight, targets, index, scale):
    heights = tuple(b.shape[0] for b in blocks)
    rows, hf = sum(heights), weight.shape[0]
    width, step = weight.shape[1], 256
    goals = rows // 128

    def goal_spec(i):
        return pl.BlockSpec((128, step), lambda j, s: (s[i], j))

    return pl.pallas_call(
        functools.partial(resid_kernel, scale, heights),
        grid_spec=pltpu.PrefetchScalarGridSpec(
            num_scalar_prefetch=1,
            grid=(width // step,),
            in_specs=[pl.BlockSpec((hf, step), lambda j, s: (0, j))]
            + [pl.BlockSpec(b.shape, lambda j, s: (0, 0)) for b in blocks]
            + [goal_spec(i) for i in range(goals)],
            out_specs=pl.BlockSpec((rows, step), lambda j, s: (0, j)),
        ),
        out_shape=jax.ShapeDtypeStruct((rows, width), jnp.bfloat16),
        compiler_params=pltpu.CompilerParams(vmem_limit_bytes=VMEM_LIMIT),
        cost_estimate=pl.CostEstimate(
            flops=2 * rows * hf * width // SHADE,
            bytes_accessed=2 * (rows * hf + hf * width + 2 * rows * width) // SHADE,
            transcendentals=0,
        ),
        name="resid",
    )(index, weight, *blocks, *([targets] * goals))


def grad_kernel(scale, n, m, more, *refs):
    blocks, resids = refs[:n], refs[n : n + m]
    grad_ref, row_ref, col_ref = refs[-3:]
    acts = jnp.concatenate([b[...] for b in blocks], axis=0)
    resid = jnp.concatenate([r[...] for r in resids], axis=0)
    grad = lax.dot_general(
        acts, resid, (((0,), (0,)), ((), ())), preferred_element_type=jnp.float32
    ) * scale
    grad_ref[...] = grad.astype(grad_ref.dtype)
    squares = grad * grad + 1e-30
    width = squares.shape[1]
    part = squares[:, :128]
    for k in range(1, width // 128):
        part = part + squares[:, k * 128 : (k + 1) * 128]
    row_ref[...] = jnp.sum(part.T, axis=0, keepdims=True)

    @pl.when(pl.program_id(0) == 0)
    def _():
        col_ref[...] = refs[n + m][...] if more else jnp.zeros_like(col_ref)

    col_ref[...] += jnp.sum(squares, axis=0, keepdims=True)


def grad_call(blocks, resids, scale, part, parts, partial=None):
    rows = sum(b.shape[0] for b in blocks)
    hf, width, step = blocks[0].shape[1], resids[0].shape[1], 1024
    steps = hf // step // parts
    base = part * steps
    given, given_specs, aliases = [], [], {}
    if partial is not None:
        grad, row, col = partial
        given = [col, grad, row]
        given_specs = [pl.BlockSpec((1, width), lambda j: (0, 0))]
        given_specs += [pl.BlockSpec(memory_space=pl.ANY)] * 2
        first = len(blocks) + len(resids)
        aliases = {first + 1: 0, first + 2: 1}
    return pl.pallas_call(
        functools.partial(grad_kernel, scale, len(blocks), len(resids), bool(given)),
        grid=(steps,),
        in_specs=[pl.BlockSpec((b.shape[0], step), lambda j: (0, j + base)) for b in blocks]
        + [pl.BlockSpec(r.shape, lambda j: (0, 0)) for r in resids]
        + given_specs,
        out_specs=[
            pl.BlockSpec((step, width), lambda j: (j + base, 0)),
            pl.BlockSpec((1, step), lambda j: (0, j + base)),
            pl.BlockSpec((1, width), lambda j: (0, 0)),
        ],
        out_shape=[
            jax.ShapeDtypeStruct((hf, width), jnp.bfloat16),
            jax.ShapeDtypeStruct((1, hf), jnp.float32),
            jax.ShapeDtypeStruct((1, width), jnp.float32),
        ],
        input_output_aliases=aliases,
        compiler_params=pltpu.CompilerParams(vmem_limit_bytes=VMEM_LIMIT),
        cost_estimate=pl.CostEstimate(
            flops=2 * rows * hf * width // parts,
            bytes_accessed=(2 * rows * (hf + width) + 2 * hf * width) // parts,
            transcendentals=0,
        ),
        name="grad",
    )(*blocks, *resids, *given)


SLOTS = 8


def merge_kernel(
    pieces, index_ref, row_state, row_a, row_b, col_state, col_sum, grad_ref, w_ref, *refs
):
    n = len(pieces)
    sources, refs = refs[:-12], refs[-12:]
    out_ref, row_next, col_next, g_buf, w_buf, a_buf, o_buf, column = refs[:8]
    g_sem, w_sem, a_sem, o_sem = refs[8:]
    rows = w_buf.shape[1]

    def at(i):
        return pl.ds(pl.multiple_of(index_ref[i] * rows, rows), rows)

    def loads(i):
        s = i % SLOTS
        array, part = pieces[i]
        return (
            pltpu.make_async_copy(grad_ref.at[at(i)], g_buf.at[s], g_sem.at[s]),
            pltpu.make_async_copy(w_ref.at[at(i)], w_buf.at[s], w_sem.at[s]),
            pltpu.make_async_copy(sources[array].at[part], a_buf.at[s], a_sem.at[s]),
        )

    def store(i):
        s = i % SLOTS
        return pltpu.make_async_copy(o_buf.at[s], out_ref.at[at(i)], o_sem.at[s])

    for i in range(SLOTS - 1):
        for copy in loads(i):
            copy.start()

    hf = w_ref.shape[0]
    row_new = decay_second * row_state[...] + (1.0 - decay_second) * (
        (row_a[...] + row_b[...]) / D
    )
    row_next[...] = row_new
    col_new = decay_second * col_state[...] + (1.0 - decay_second) * (col_sum[...] / hf)
    col_next[...] = col_new
    turned = lax.rsqrt(row_new).T
    for i in range(turned.shape[1]):
        column[i * 128 : (i + 1) * 128, :] = turned[:, i : i + 1]
    colfac = (0.5 * inner_rate) * lax.rsqrt(col_new) * jnp.sqrt(jnp.mean(row_new))

    for i in range(n):
        if i + SLOTS - 1 < n:
            for copy in loads(i + SLOTS - 1):
                copy.start()
        for copy in loads(i):
            copy.wait()
        s = i % SLOTS
        if i >= SLOTS:
            store(i - SLOTS).wait()
        w = w_buf[s].astype(jnp.float32)
        a = a_buf[s].astype(jnp.float32)
        keep = 0.5 * (1.0 - inner_rate * weight_decay)
        step = g_buf[s].astype(jnp.float32) * column[at(i), :] * colfac
        o_buf[s] = (keep * w - step + 0.5 * a).astype(jnp.bfloat16)
        store(i).start()
    for i in range(n - SLOTS, n):
        store(i).wait()


def merge_call(sources, pieces, index, row_state, row_a, row_b, col_state, col_sum, grad, weight):
    rows, width = 96, weight.shape[1]
    vmem = pl.BlockSpec(memory_space=pltpu.VMEM)
    anywhere = pl.BlockSpec(memory_space=pl.ANY)
    return pl.pallas_call(
        functools.partial(merge_kernel, pieces),
        in_specs=[pl.BlockSpec(memory_space=pltpu.SMEM)]
        + [vmem] * 5
        + [anywhere] * (2 + len(sources)),
        out_specs=[anywhere, vmem, vmem],
        out_shape=[
            jax.ShapeDtypeStruct(weight.shape, jnp.bfloat16),
            jax.ShapeDtypeStruct(row_state.shape, jnp.float32),
            jax.ShapeDtypeStruct(col_state.shape, jnp.float32),
        ],
        scratch_shapes=[pltpu.VMEM((SLOTS, rows, width), jnp.bfloat16)] * 4
        + [pltpu.VMEM((weight.shape[0], 1), jnp.float32)]
        + [pltpu.SemaphoreType.DMA((SLOTS,))] * 4,
        compiler_params=pltpu.CompilerParams(vmem_limit_bytes=VMEM_LIMIT),
        cost_estimate=pl.CostEstimate(
            flops=8 * weight.size, bytes_accessed=8 * weight.size, transcendentals=0
        ),
        name="merge",
    )(index, row_state, row_a, row_b, col_state, col_sum, grad, weight, *sources)


def body(activations, targets, replica_weight, row_state, col_state, anchor, momentum):
    weight = replica_weight[0]
    hf, width = weight.shape
    island = targets.shape[0]
    inv_root = 1.0 / float(hf) ** 0.5
    mesh_size = {"zl": NZ, "x": NX, "c": NC, "zh": NH, "y": NY}
    zl, x, c = lax.axis_index("zl"), lax.axis_index("x"), lax.axis_index("c")
    zh, y = lax.axis_index("zh"), lax.axis_index("y")
    rows = hf // (NZ * NX * NC)

    def send(block, axis, k, what):
        with jax.named_scope(what):
            return lax.ppermute(block, axis, ring(mesh_size[axis], k))

    side = 1 - 2 * c

    def turn(block, axis, k, what):
        n = mesh_size[axis]
        axes = ("x", "c") if axis == "x" else ("c", axis)

        def place(i, j):
            return i * NC + j if axis == "x" else j * n + i

        pairs = [
            (place(i, j), place((i + (k if j == 0 else -k)) % n, j))
            for i in range(n)
            for j in range(NC)
        ]
        with jax.named_scope(what):
            return lax.ppermute(block, axes, pairs)

    grid = weight.reshape(NZ, NX, NC, rows, width)
    theirs = lax.dynamic_index_in_dim(grid, 1 - c, 2, keepdims=False)
    pair = send(theirs, "c", 1, "sum_core")
    near = turn(activations, "y", 1, "acts_near")
    zown = send(activations, "zh", 1, "acts_zown")

    half_type = jnp.bfloat16
    here, ahead, behind, across = pieces_call(
        grid, pair, c, [(x + dx + NX) % NX for dx in (0, side, -side, 2)]
    )
    back = turn(activations, "y", -1, "acts_back")
    cut = 80
    far0 = turn(after(near, back)[:cut], "y", 1, "acts_far0")
    far1 = turn(after(near, far0)[cut:], "y", 1, "acts_far1")
    got_near = turn(ahead, "x", 1, "sum_near")
    got_back = turn(behind, "x", -1, "sum_back")
    got_far = send(across, "x", 2, "sum_far")
    def goal(dz, dy):
        return (zh + dz) % NH * NY + (y + dy + NY) % NY

    parts = [
        (
            [activations, near, back],
            [goal(0, 0), goal(0, -side), goal(0, side)],
        ),
        (
            [far0, far1],
            [goal(0, 2), goal(1, 0), goal(1, -side), goal(1, side)],
        ),
        (
            [],
            [goal(1, 2)],
        ),
    ]
    def resid_of(g, *wait):
        held, goals = parts[g]
        index = after(jnp.stack(goals).astype(jnp.int32), *wait)
        return resid_call(held, weight, targets, index, inv_root)

    resids = [resid_of(0)]
    z_order = (2, 1, 3, 0)
    *z_sent, share = total_call(
        (here, got_near, got_back, got_far),
        (corner(zown, resids[0]),),
        jnp.stack([(zl + k) % NZ for k in z_order]).astype(jnp.int32),
    )
    z_sent = [after(p, far0) for p in z_sent]
    z_got = [send(p, "zl", k, "sum_z%d" % k) for p, k in zip(z_sent, z_order)]
    znear = turn(after(zown, *z_sent), "y", 1, "acts_znear")
    zback = turn(after(zown, *z_sent), "y", -1, "acts_zback")
    zfar = turn(after(znear, *z_got), "y", 1, "acts_zfar")
    for got in z_got:
        share = share + got.astype(jnp.float32)
    parts[1][0].extend((zown, znear, zback))
    parts[2][0].append(zfar)
    share = after(share, znear)

    outer_grad = anchor - share / (NZ * NX * NC)
    momentum_next = outer_momentum * momentum + outer_grad
    anchor_next = anchor - outer_rate * (outer_grad + outer_momentum * momentum_next)
    half = anchor_next.astype(jnp.bfloat16)[None]

    over_z = [send(half, "zl", k, "new_z%d" % k) for k in (1, 2, 3)]
    resids += [resid_of(1, half), resid_of(2, half)]
    over_z = [after(o, *resids[:2]) for o in over_z]
    held = jnp.concatenate([half] + over_z)
    new_near = turn(held, "x", 1, "new_near")
    new_back = turn(held, "x", -1, "new_back")
    blocks = [b for blocks, _ in parts for b in blocks]
    scale = inv_root / island
    grad, row_sum, col_sum = grad_call(blocks, resids, scale, 0, 1)
    row_sum = row_sum.reshape(hf // 128, 128)
    row_a = row_sum
    for k in (1, 2, 3):
        row_a = row_a + send(row_sum, "y", k, "row_y")
    row_b = send(row_a, "zh", 1, "row_z")

    new_far = turn(after(new_near, new_back, row_sum), "x", 1, "new_far")
    sources, pieces, places = [], [], []
    late = ((held, 0), (new_near, -side), (new_back, side), (new_far, 2))
    for i, (block, origin) in enumerate(late):
        for swap in (0, 1):
            from_c = 1 - c if swap else c
            from_x = (x + (-origin if swap else origin) + NX) % NX
            for k in range(NZ):
                pieces.append((len(sources), k))
                places.append(((zl + NZ - k) % NZ * NX + from_x) * NC + from_c)
            sources.append(send(after(block, row_b if i == 3 else row_a), "c", 1, "new_core") if swap else block)
    places = jnp.stack(places).astype(jnp.int32)

    merged, row_new, col_new = merge_call(
        sources,
        tuple(pieces),
        places,
        row_state.reshape(row_sum.shape),
        row_a,
        row_b,
        col_state,
        col_sum,
        grad,
        weight,
    )
    return (merged[None], row_new.reshape(row_state.shape), col_new, anchor_next, momentum_next)


def solution(mesh):
    fine = Mesh(
        mesh.devices.reshape(NZ, NX, NC, NH, NY), ("zl", "x", "c", "zh", "y")
    )
    rep, fsdp = ("zl", "x", "c"), ("zh", "y")
    placed = (
        P(rep + fsdp, None),
        P(rep, fsdp),
        P(rep, None, fsdp),
        P(rep, None),
        P(rep, fsdp),
        P(rep, fsdp),
        P(rep, fsdp),
    )
    return jax.shard_map(
        body,
        mesh=fine,
        in_specs=placed,
        out_specs=(
            P(rep, None, fsdp),
            P(rep, None),
            P(rep, fsdp),
            P(rep, fsdp),
            P(rep, fsdp),
        ),
        check_vma=False,
    )
```

```python
import functools

import jax
import jax.numpy as jnp
from jax import lax
from jax.experimental import pallas as pl
from jax.experimental.pallas import tpu as pltpu
from jax.sharding import Mesh, PartitionSpec as P

D = 6144
decay_second = 0.95
inner_rate = 0.25
weight_decay = 0.1
outer_rate = 0.7
outer_momentum = 0.9

NZ, NX, NC, NH, NY = 4, 4, 2, 2, 4
VMEM_LIMIT = 60 * 1024 * 1024
SMALL_LIMIT = 12 * 1024 * 1024
SHADE = 16


def after(value, *others):
    return lax.optimization_barrier((value, *others))[0]


def ring(n, k):
    return [(i, (i + k) % n) for i in range(n)]


def pieces_kernel(n, index_ref, *refs):
    mine, pair, outs = refs[:n], refs[n : 2 * n], refs[2 * n :]
    for a, b, out in zip(mine, pair, outs):
        total = a[0, 0, 0].astype(jnp.float32) + b[0, 0].astype(jnp.float32)
        out[0] = total.astype(out.dtype)


def pieces_call(grid, pair, c, columns):
    nz, nx, _, rows, width = grid.shape
    n = len(columns)
    index = jnp.stack([c, *columns]).astype(jnp.int32)

    def mine_spec(i):
        return pl.BlockSpec((1, 1, 1, rows, width), lambda j, s: (j, s[i + 1], s[0], 0, 0))

    def pair_spec(i):
        return pl.BlockSpec((1, 1, rows, width), lambda j, s: (j, s[i + 1], 0, 0))

    return pl.pallas_call(
        functools.partial(pieces_kernel, n),
        grid_spec=pltpu.PrefetchScalarGridSpec(
            num_scalar_prefetch=1,
            grid=(nz,),
            in_specs=[mine_spec(i) for i in range(n)] + [pair_spec(i) for i in range(n)],
            out_specs=[pl.BlockSpec((1, rows, width), lambda j, s: (j, 0, 0))] * n,
        ),
        out_shape=[jax.ShapeDtypeStruct((nz, rows, width), jnp.bfloat16)] * n,
        compiler_params=pltpu.CompilerParams(vmem_limit_bytes=SMALL_LIMIT),
        cost_estimate=pl.CostEstimate(
            flops=0, bytes_accessed=400 * 1000 * 1000, transcendentals=0
        ),
        name="pieces",
    )(index, *([grid] * n), *([pair] * n))


def corner_kernel(in_ref, waited_ref, out_ref):
    out_ref[...] = in_ref[...]


def corner(array, waited):
    block = pl.BlockSpec((16, 128), lambda i: (0, 0))
    return pl.pallas_call(
        corner_kernel,
        grid=(1,),
        in_specs=[block, pl.BlockSpec(memory_space=pl.ANY)],
        out_specs=block,
        out_shape=jax.ShapeDtypeStruct((16, 128), array.dtype),
        compiler_params=pltpu.CompilerParams(vmem_limit_bytes=SMALL_LIMIT),
        name="corner",
    )(array, waited)


def total_kernel(index_ref, here, near, back, far, *refs):
    a_ref, b_ref, c_ref, own_ref = refs[-4:]
    step = pl.program_id(0)
    total = here[0].astype(jnp.float32)
    for array in (near, back, far):
        total = total + array[0].astype(jnp.float32)

    for i, out in enumerate((a_ref, b_ref, c_ref, own_ref)):

        @pl.when(step == i)
        def _(out=out):
            out[...] = total.astype(out.dtype)


def total_call(arrays, waited, order):
    nz, rows, width = arrays[0].shape
    block = pl.BlockSpec((1, rows, width), lambda j, s: (s[j], 0, 0))
    out = pl.BlockSpec((rows, width), lambda j, s: (0, 0))
    half = jax.ShapeDtypeStruct((rows, width), jnp.bfloat16)
    return pl.pallas_call(
        total_kernel,
        grid_spec=pltpu.PrefetchScalarGridSpec(
            num_scalar_prefetch=1,
            grid=(nz,),
            in_specs=[block] * 4 + [pl.BlockSpec(memory_space=pl.ANY)] * len(waited),
            out_specs=[out] * 4,
        ),
        out_shape=[half] * 3 + [jax.ShapeDtypeStruct((rows, width), jnp.float32)],
        compiler_params=pltpu.CompilerParams(vmem_limit_bytes=SMALL_LIMIT),
        name="total",
    )(order, *arrays, *waited)


def resid_kernel(scale, heights, index_ref, w_ref, *refs):
    n = len(heights)
    blocks, goals, out_ref = refs[:n], refs[n:-1], refs[-1]
    acts = jnp.concatenate([b[...] for b in blocks], axis=0)
    output = jnp.dot(acts, w_ref[...], preferred_element_type=jnp.float32) * scale
    goal = jnp.concatenate([g[...] for g in goals], axis=0).astype(jnp.float32)
    out_ref[...] = (output - goal).astype(jnp.bfloat16)


def resid_call(blocks, weight, targets, index, scale):
    heights = tuple(b.shape[0] for b in blocks)
    rows, hf = sum(heights), weight.shape[0]
    width, step = weight.shape[1], 256
    goals = rows // 128

    def goal_spec(i):
        return pl.BlockSpec((128, step), lambda j, s: (s[i], j))

    return pl.pallas_call(
        functools.partial(resid_kernel, scale, heights),
        grid_spec=pltpu.PrefetchScalarGridSpec(
            num_scalar_prefetch=1,
            grid=(width // step,),
            in_specs=[pl.BlockSpec((hf, step), lambda j, s: (0, j))]
            + [pl.BlockSpec(b.shape, lambda j, s: (0, 0)) for b in blocks]
            + [goal_spec(i) for i in range(goals)],
            out_specs=pl.BlockSpec((rows, step), lambda j, s: (0, j)),
        ),
        out_shape=jax.ShapeDtypeStruct((rows, width), jnp.bfloat16),
        compiler_params=pltpu.CompilerParams(vmem_limit_bytes=VMEM_LIMIT),
        cost_estimate=pl.CostEstimate(
            flops=2 * rows * hf * width // SHADE,
            bytes_accessed=2 * (rows * hf + hf * width + 2 * rows * width) // SHADE,
            transcendentals=0,
        ),
        name="resid",
    )(index, weight, *blocks, *([targets] * goals))


def grad_kernel(scale, n, m, more, *refs):
    blocks, resids = refs[:n], refs[n : n + m]
    grad_ref, row_ref, col_ref = refs[-3:]
    acts = jnp.concatenate([b[...] for b in blocks], axis=0)
    resid = jnp.concatenate([r[...] for r in resids], axis=0)
    grad = lax.dot_general(
        acts, resid, (((0,), (0,)), ((), ())), preferred_element_type=jnp.float32
    ) * scale
    grad_ref[...] = grad.astype(grad_ref.dtype)
    squares = grad * grad + 1e-30
    width = squares.shape[1]
    part = squares[:, :128]
    for k in range(1, width // 128):
        part = part + squares[:, k * 128 : (k + 1) * 128]
    row_ref[...] = jnp.sum(part.T, axis=0, keepdims=True)

    @pl.when(pl.program_id(0) == 0)
    def _():
        col_ref[...] = refs[n + m][...] if more else jnp.zeros_like(col_ref)

    col_ref[...] += jnp.sum(squares, axis=0, keepdims=True)


def grad_call(blocks, resids, scale, part, parts, partial=None):
    rows = sum(b.shape[0] for b in blocks)
    hf, width, step = blocks[0].shape[1], resids[0].shape[1], 1024
    steps = hf // step // parts
    base = part * steps
    given, given_specs, aliases = [], [], {}
    if partial is not None:
        grad, row, col = partial
        given = [col, grad, row]
        given_specs = [pl.BlockSpec((1, width), lambda j: (0, 0))]
        given_specs += [pl.BlockSpec(memory_space=pl.ANY)] * 2
        first = len(blocks) + len(resids)
        aliases = {first + 1: 0, first + 2: 1}
    return pl.pallas_call(
        functools.partial(grad_kernel, scale, len(blocks), len(resids), bool(given)),
        grid=(steps,),
        in_specs=[pl.BlockSpec((b.shape[0], step), lambda j: (0, j + base)) for b in blocks]
        + [pl.BlockSpec(r.shape, lambda j: (0, 0)) for r in resids]
        + given_specs,
        out_specs=[
            pl.BlockSpec((step, width), lambda j: (j + base, 0)),
            pl.BlockSpec((1, step), lambda j: (0, j + base)),
            pl.BlockSpec((1, width), lambda j: (0, 0)),
        ],
        out_shape=[
            jax.ShapeDtypeStruct((hf, width), jnp.bfloat16),
            jax.ShapeDtypeStruct((1, hf), jnp.float32),
            jax.ShapeDtypeStruct((1, width), jnp.float32),
        ],
        input_output_aliases=aliases,
        compiler_params=pltpu.CompilerParams(vmem_limit_bytes=VMEM_LIMIT),
        cost_estimate=pl.CostEstimate(
            flops=2 * rows * hf * width // parts,
            bytes_accessed=(2 * rows * (hf + width) + 2 * hf * width) // parts,
            transcendentals=0,
        ),
        name="grad",
    )(*blocks, *resids, *given)


SLOTS = 8


def merge_kernel(
    pieces, index_ref, row_state, row_a, row_b, col_state, col_sum, grad_ref, w_ref, *refs
):
    n = len(pieces)
    sources, refs = refs[:-12], refs[-12:]
    out_ref, row_next, col_next, g_buf, w_buf, a_buf, o_buf, column = refs[:8]
    g_sem, w_sem, a_sem, o_sem = refs[8:]
    rows = w_buf.shape[1]

    def at(i):
        return pl.ds(pl.multiple_of(index_ref[i] * rows, rows), rows)

    def loads(i):
        s = i % SLOTS
        array, part = pieces[i]
        return (
            pltpu.make_async_copy(grad_ref.at[at(i)], g_buf.at[s], g_sem.at[s]),
            pltpu.make_async_copy(w_ref.at[at(i)], w_buf.at[s], w_sem.at[s]),
            pltpu.make_async_copy(sources[array].at[part], a_buf.at[s], a_sem.at[s]),
        )

    def store(i):
        s = i % SLOTS
        return pltpu.make_async_copy(o_buf.at[s], out_ref.at[at(i)], o_sem.at[s])

    for i in range(SLOTS - 1):
        for copy in loads(i):
            copy.start()

    hf = w_ref.shape[0]
    row_new = decay_second * row_state[...] + (1.0 - decay_second) * (
        (row_a[...] + row_b[...]) / D
    )
    row_next[...] = row_new
    col_new = decay_second * col_state[...] + (1.0 - decay_second) * (col_sum[...] / hf)
    col_next[...] = col_new
    turned = lax.rsqrt(row_new).T
    for i in range(turned.shape[1]):
        column[i * 128 : (i + 1) * 128, :] = turned[:, i : i + 1]
    colfac = (0.5 * inner_rate) * lax.rsqrt(col_new) * jnp.sqrt(jnp.mean(row_new))

    for i in range(n):
        if i + SLOTS - 1 < n:
            for copy in loads(i + SLOTS - 1):
                copy.start()
        for copy in loads(i):
            copy.wait()
        s = i % SLOTS
        if i >= SLOTS:
            store(i - SLOTS).wait()
        w = w_buf[s].astype(jnp.float32)
        a = a_buf[s].astype(jnp.float32)
        keep = 0.5 * (1.0 - inner_rate * weight_decay)
        step = g_buf[s].astype(jnp.float32) * column[at(i), :] * colfac
        o_buf[s] = (keep * w - step + 0.5 * a).astype(jnp.bfloat16)
        store(i).start()
    for i in range(n - SLOTS, n):
        store(i).wait()


def merge_call(sources, pieces, index, row_state, row_a, row_b, col_state, col_sum, grad, weight):
    rows, width = 96, weight.shape[1]
    vmem = pl.BlockSpec(memory_space=pltpu.VMEM)
    anywhere = pl.BlockSpec(memory_space=pl.ANY)
    return pl.pallas_call(
        functools.partial(merge_kernel, pieces),
        in_specs=[pl.BlockSpec(memory_space=pltpu.SMEM)]
        + [vmem] * 5
        + [anywhere] * (2 + len(sources)),
        out_specs=[anywhere, vmem, vmem],
        out_shape=[
            jax.ShapeDtypeStruct(weight.shape, jnp.bfloat16),
            jax.ShapeDtypeStruct(row_state.shape, jnp.float32),
            jax.ShapeDtypeStruct(col_state.shape, jnp.float32),
        ],
        scratch_shapes=[pltpu.VMEM((SLOTS, rows, width), jnp.bfloat16)] * 4
        + [pltpu.VMEM((weight.shape[0], 1), jnp.float32)]
        + [pltpu.SemaphoreType.DMA((SLOTS,))] * 4,
        compiler_params=pltpu.CompilerParams(vmem_limit_bytes=VMEM_LIMIT),
        cost_estimate=pl.CostEstimate(
            flops=8 * weight.size, bytes_accessed=8 * weight.size, transcendentals=0
        ),
        name="merge",
    )(index, row_state, row_a, row_b, col_state, col_sum, grad, weight, *sources)


def body(activations, targets, replica_weight, row_state, col_state, anchor, momentum):
    weight = replica_weight[0]
    hf, width = weight.shape
    island = targets.shape[0]
    inv_root = 1.0 / float(hf) ** 0.5
    mesh_size = {"zl": NZ, "x": NX, "c": NC, "zh": NH, "y": NY}
    zl, x, c = lax.axis_index("zl"), lax.axis_index("x"), lax.axis_index("c")
    zh, y = lax.axis_index("zh"), lax.axis_index("y")
    rows = hf // (NZ * NX * NC)

    def send(block, axis, k, what):
        with jax.named_scope(what):
            return lax.ppermute(block, axis, ring(mesh_size[axis], k))

    side = 1 - 2 * c

    def turn(block, axis, k, what):
        n = mesh_size[axis]
        axes = ("x", "c") if axis == "x" else ("c", axis)

        def place(i, j):
            return i * NC + j if axis == "x" else j * n + i

        pairs = [
            (place(i, j), place((i + (k if j == 0 else -k)) % n, j))
            for i in range(n)
            for j in range(NC)
        ]
        with jax.named_scope(what):
            return lax.ppermute(block, axes, pairs)

    grid = weight.reshape(NZ, NX, NC, rows, width)
    theirs = lax.dynamic_index_in_dim(grid, 1 - c, 2, keepdims=False)
    pair = send(theirs, "c", 1, "sum_core")
    near = turn(activations, "y", 1, "acts_near")
    zown = send(activations, "zh", 1, "acts_zown")

    half_type = jnp.bfloat16
    here, ahead, behind, across = pieces_call(
        grid, pair, c, [(x + dx + NX) % NX for dx in (0, side, -side, 2)]
    )
    back = turn(activations, "y", -1, "acts_back")
    cut = 80
    far0 = turn(after(near, back)[:cut], "y", 1, "acts_far0")
    far1 = turn(after(near, far0)[cut:], "y", 1, "acts_far1")
    got_near = turn(ahead, "x", 1, "sum_near")
    got_back = turn(behind, "x", -1, "sum_back")
    got_far = send(across, "x", 2, "sum_far")
    def goal(dz, dy):
        return (zh + dz) % NH * NY + (y + dy + NY) % NY

    parts = [
        (
            [activations, near, back],
            [goal(0, 0), goal(0, -side), goal(0, side)],
        ),
        (
            [far0, far1],
            [goal(0, 2), goal(1, 0), goal(1, -side), goal(1, side)],
        ),
        (
            [],
            [goal(1, 2)],
        ),
    ]
    def resid_of(g, *wait):
        held, goals = parts[g]
        index = after(jnp.stack(goals).astype(jnp.int32), *wait)
        return resid_call(held, weight, targets, index, inv_root)

    resids = [resid_of(0)]
    z_order = (2, 1, 3, 0)
    *z_sent, share = total_call(
        (here, got_near, got_back, got_far),
        (corner(zown, resids[0]),),
        jnp.stack([(zl + k) % NZ for k in z_order]).astype(jnp.int32),
    )
    z_sent = [after(p, far0) for p in z_sent]
    z_got = [send(p, "zl", k, "sum_z%d" % k) for p, k in zip(z_sent, z_order)]
    znear = turn(after(zown, *z_sent), "y", 1, "acts_znear")
    zback = turn(after(zown, *z_sent), "y", -1, "acts_zback")
    zfar = turn(after(znear, *z_got), "y", 1, "acts_zfar")
    for got in z_got:
        share = share + got.astype(jnp.float32)
    parts[1][0].extend((zown, znear, zback))
    parts[2][0].append(zfar)
    share = after(share, far0)

    outer_grad = anchor - share / (NZ * NX * NC)
    momentum_next = outer_momentum * momentum + outer_grad
    anchor_next = anchor - outer_rate * (outer_grad + outer_momentum * momentum_next)
    half = anchor_next.astype(jnp.bfloat16)[None]

    over_z = [send(half, "zl", k, "new_z%d" % k) for k in (1, 2, 3)]
    resids += [resid_of(1, half), resid_of(2, half)]
    over_z = [after(o, *resids[:2]) for o in over_z]
    held = jnp.concatenate([half] + over_z)
    new_near = turn(held, "x", 1, "new_near")
    new_back = turn(held, "x", -1, "new_back")
    blocks = [b for blocks, _ in parts for b in blocks]
    scale = inv_root / island
    grad, row_sum, col_sum = grad_call(blocks, resids, scale, 0, 1)
    row_sum = row_sum.reshape(hf // 128, 128)
    row_a = row_sum
    for k in (1, 2, 3):
        row_a = row_a + send(row_sum, "y", k, "row_y")
    row_b = send(row_a, "zh", 1, "row_z")

    new_far = turn(after(new_near, new_back, row_sum), "x", 1, "new_far")
    sources, pieces, places = [], [], []
    late = ((held, 0), (new_near, -side), (new_back, side), (new_far, 2))
    for i, (block, origin) in enumerate(late):
        for swap in (0, 1):
            from_c = 1 - c if swap else c
            from_x = (x + (-origin if swap else origin) + NX) % NX
            for k in range(NZ):
                pieces.append((len(sources), k))
                places.append(((zl + NZ - k) % NZ * NX + from_x) * NC + from_c)
            sources.append(send(after(block, row_b if i == 3 else row_a), "c", 1, "new_core") if swap else block)
    places = jnp.stack(places).astype(jnp.int32)

    merged, row_new, col_new = merge_call(
        sources,
        tuple(pieces),
        places,
        row_state.reshape(row_sum.shape),
        row_a,
        row_b,
        col_state,
        col_sum,
        grad,
        weight,
    )
    return (merged[None], row_new.reshape(row_state.shape), col_new, anchor_next, momentum_next)


def solution(mesh):
    fine = Mesh(
        mesh.devices.reshape(NZ, NX, NC, NH, NY), ("zl", "x", "c", "zh", "y")
    )
    rep, fsdp = ("zl", "x", "c"), ("zh", "y")
    placed = (
        P(rep + fsdp, None),
        P(rep, fsdp),
        P(rep, None, fsdp),
        P(rep, None),
        P(rep, fsdp),
        P(rep, fsdp),
        P(rep, fsdp),
    )
    return jax.shard_map(
        body,
        mesh=fine,
        in_specs=placed,
        out_specs=(
            P(rep, None, fsdp),
            P(rep, None),
            P(rep, fsdp),
            P(rep, fsdp),
            P(rep, fsdp),
        ),
        check_vma=False,
    )
```
